32 devices in a mesh: groups: 2 (over y), expert: 16 (over z, x, core).
Axes of the slice: x: 2, y: 2, z: 4, core: 2. Of those that a mesh axis runs over, the one named last changes fastest.
Arguments:
- tokens: bfloat16 [4096, 3584], P(('groups', 'expert')), parts along dimension 0, may hold values from -6 to 6
- grad_out: bfloat16 [4096, 3584], P(('groups', 'expert')), parts along dimension 0, may hold values from -6 to 6
- route_weight: bfloat16 [4096, 1], P(('groups', 'expert')), parts along dimension 0, may hold values from 0.099609375 to 1
- expert_ids: int32 [4096, 1], P(('groups', 'expert')), parts along dimension 0, may hold values from 0 to 1; in each aligned block of 128 rows (0 to 127, 128 to 255, ...) at most 80 rows name the same one
- w_gate: bfloat16 [16, 3584, 128], P('expert'), may hold values from -0.09375 to 0.09375
- w_up: bfloat16 [16, 3584, 128], P('expert'), may hold values from -0.09375 to 0.09375
- w_down: bfloat16 [16, 128, 3584], P('expert'), may hold values from -0.1875 to 0.1875
Outputs:
- grad_tokens: bfloat16 [4096, 3584], P(('groups', 'expert')), parts along dimension 0
- grad_combine: float32 [4096, 1], P(('groups', 'expert')), parts along dimension 0
- grad_gate: bfloat16 [32, 3584, 128], P(('groups', 'expert')), parts along dimension 0
- grad_up: bfloat16 [32, 3584, 128], P(('groups', 'expert')), parts along dimension 0
- grad_down: bfloat16 [32, 128, 3584], P(('groups', 'expert')), parts along dimension 0
The draws below stay inside these ranges and needn't reach their ends.
There are 2 independent parts, one for each index of `groups`. The reference program is written for one: setup_inputs(seed, part) draws one part's arguments, and reference() takes and returns one part's arrays. A program takes and returns all parts, laid end to end along the dimension named above; an argument that names none is the same for every part. Nothing has to cross between parts.
Inputs may be any that keep to these rules, and one draw needn't show every extreme that they name: `expert_ids`: each row names 1 different experts; within the 128 rows of one device no expert is named more than 80 times, a bound that some block reaches.
All inputs are finite; a program needn't handle non-finite values.
Results may differ from the reference program's by a relative error of at most 0.008.
Values may be sent and summed in bfloat16 or wider, within the bound.
No kernel may reach another device: no remote copies, remote signals or barrier semaphores. Data moves between devices by JAX's collectives and lax.ppermute only.
A program may use at most 192 MiB of HBM per device.

```python
import math
import jax
import jax.numpy as jnp
import numpy as np
from jax import lax

D = 3584
EXP_HID = 1024
SPLIT = 8
TOP = 1
TOK_DEV = 128
EXPERTS = 2
HID_DEV = 128
CAP = 80
TOKENS = 2048
N_EXPERT = 16


def block_scale(stream_key, extent, cuts, least, largest):
    loudness = 1.0
    for dim, shards_of in cuts:
        draws = jax.random.uniform(jax.random.fold_in(jax.random.fold_in(stream_key, 6), dim), (shards_of,), jnp.float32, least / len(cuts), largest / len(cuts))
        loudness = loudness * jnp.repeat(jnp.exp(draws), extent[dim] // shards_of).reshape((-1,) + (1,) * (len(extent) - 1 - dim))
    return loudness


def deal_out(stream_key, own, number, rows, amount, top, limit, slope):
    order = jax.random.permutation(stream_key, amount)
    heavy_load, common = shares(amount, rows * top, limit, slope, True), shares(amount, rows * top, limit, slope, False)
    places = jnp.arange(amount)

    def named(tallies, rotation):
        used = int((tallies > 0).sum())
        fixed = max(1, used // 4)
        passed = fixed + (places - fixed + rotation * (used - fixed)) % max(1, amount - fixed)
        return jnp.zeros((amount,), jnp.int32).at[order[jnp.where(places < fixed, places, passed)]].set(jnp.asarray(tallies, jnp.int32))

    tallies = jnp.where(number % 4 == 0, named(heavy_load, number // 4), named(common, number - number // 4 - 1))
    mixed = jax.random.permutation(jax.random.fold_in(own, 3), amount)
    donor, taker = mixed[0:amount // 2 * 2:2], mixed[1:amount // 2 * 2:2]
    slack = jnp.minimum(tallies[donor] - 1, limit - tallies[taker]) // 2
    slack = jnp.where((donor == order[0]) | (taker == order[0]) | (tallies[taker] == 0), 0, jnp.maximum(slack, 0))
    passed = jax.random.randint(jax.random.fold_in(own, 4), (amount // 2,), 0, 1 << 20) % (slack + 1)
    tallies = tallies.at[donor].add(-passed).at[taker].add(passed)
    members = jnp.searchsorted(jnp.cumsum(tallies), jnp.arange(rows * top), side="right").astype(jnp.int32)
    grid = members.reshape(top, rows).T
    grid = grid[jax.random.permutation(jax.random.fold_in(own, 1), rows)]
    rotation = jax.random.randint(jax.random.fold_in(own, 2), (rows, 1), 0, top)
    return jnp.take_along_axis(grid, (jnp.arange(top)[None, :] + rotation) % top, axis=1)


def shares(amount, total, reach, skew, full):
    portions = [(1 << 20) // math.isqrt(grade ** skew) + 1 for grade in range(1, amount + 1)]
    largest = reach if full else min(reach, max(-(-total // amount), total * portions[0] // sum(portions)))
    least = 1 if total - largest >= amount - 1 else 0
    counts, surplus = [largest] + [least] * (amount - 1), total - largest - least * (amount - 1)
    while surplus > 0:
        free = [i for i in range(1, amount) if counts[i] < largest] or [i for i in range(1, amount) if counts[i] < reach]
        whole, remaining = sum([portions[i] for i in free]), surplus
        for i in free:
            extra = min(reach - counts[i], max(1, remaining * portions[i] // whole), surplus)
            counts[i] = counts[i] + extra
            surplus = surplus - extra
    return np.array(counts)


def noise(key, dims, scale, bound, split=(), held_as=jnp.bfloat16):
    factor_of = block_scale(key, dims, split, -0.22, 0.18) if split else 1.0
    result = jax.random.normal(key, dims, jnp.float32) * scale * factor_of
    return jnp.minimum(jnp.maximum(result, -bound), bound).astype(held_as)


def setup_inputs(seed: int = 0, part: int = 0) -> dict:
    key_list = jax.random.split(jax.random.key(seed), 8)
    part_splits = jax.random.split(jax.random.fold_in(key_list[7], part), 8)
    tokens = noise(part_splits[0], (TOKENS, D), 1.0, 6.0, ((0, 16),))
    grad_out = noise(part_splits[1], (TOKENS, D), 1.0, 6.0, ((0, 16),))
    route_weight = jnp.clip(0.099609375 + 0.9003906 * jax.random.uniform(part_splits[2], (TOKENS, TOP), jnp.float32) ** block_scale(part_splits[2], (TOKENS, TOP), ((0, 16),), -0.2, 0.2), 0.099609375, 1.0).astype(jnp.bfloat16)
    expert_ids_keys = jax.random.split(jax.random.fold_in(part_splits[3], 1), TOKENS // TOK_DEV)
    expert_ids_turns = jax.random.permutation(jax.random.fold_in(part_splits[3], 3), TOKENS // TOK_DEV)
    expert_ids = jax.vmap(lambda own, number: deal_out(jax.random.fold_in(part_splits[3], 2), own, number, TOK_DEV, EXPERTS, TOP, CAP, 2))(expert_ids_keys, expert_ids_turns).reshape((TOKENS, TOP))
    w_gate = noise(key_list[4], (EXPERTS * SPLIT, D, HID_DEV), D ** -0.5, 0.09375, ((0, 16),))
    w_up = noise(key_list[5], (EXPERTS * SPLIT, D, HID_DEV), D ** -0.5, 0.09375, ((0, 16),))
    w_down = noise(key_list[6], (EXPERTS * SPLIT, HID_DEV, D), EXP_HID ** -0.5, 0.1875, ((0, 16),))
    return dict(tokens=tokens, grad_out=grad_out, route_weight=route_weight, expert_ids=expert_ids, w_gate=w_gate, w_up=w_up, w_down=w_down)


def slot_positions(block_ids, experts):
    flat_ids = block_ids.reshape(-1)
    onehot = (flat_ids[:, None] == jnp.arange(experts, dtype=jnp.int32)[None, :]).astype(jnp.int32)
    before = jnp.cumsum(onehot, axis=0) - onehot
    return flat_ids, jnp.sum(before * onehot, axis=1)


def expert_pass(rows_x, rows_dy, rows_weight, gate_mat, up_mat, down_mat):
    row_count = rows_x.shape[0]
    gate_pre = jnp.dot(rows_x, gate_mat, preferred_element_type=jnp.float32)
    up_pre = jnp.dot(rows_x, up_mat, preferred_element_type=jnp.float32)
    sigma = jax.nn.sigmoid(gate_pre)
    act_silu = gate_pre * sigma
    hidden = act_silu * up_pre
    grad_hidden = lax.dot_general(rows_dy, down_mat, (((1,), (1,)), ((), ())), preferred_element_type=jnp.float32)
    prob_part = jnp.sum((hidden * grad_hidden).reshape(row_count, SPLIT, HID_DEV), axis=2).astype(jnp.bfloat16)
    row_scale = rows_weight.astype(jnp.float32)[:, None]
    grad_act = row_scale * grad_hidden
    grad_gpre = (grad_act * up_pre * sigma * (1.0 + gate_pre * (1.0 - sigma))).astype(jnp.bfloat16)
    grad_upre = (grad_act * act_silu).astype(jnp.bfloat16)
    gate_split = gate_mat.astype(jnp.float32).reshape(D, SPLIT, HID_DEV)
    up_split = up_mat.astype(jnp.float32).reshape(D, SPLIT, HID_DEV)
    rows_part = jnp.einsum('rsh,dsh->srd', grad_gpre.astype(jnp.float32).reshape(row_count, SPLIT, HID_DEV), gate_split)
    rows_part = rows_part + jnp.einsum('rsh,dsh->srd', grad_upre.astype(jnp.float32).reshape(row_count, SPLIT, HID_DEV), up_split)
    rows_part = rows_part.astype(jnp.bfloat16)
    hidden_bf = hidden.astype(jnp.bfloat16)
    scaled_dy = (row_scale * rows_dy.astype(jnp.float32)).astype(jnp.bfloat16)
    grad_gate = lax.dot_general(rows_x, grad_gpre, (((0,), (0,)), ((), ())), preferred_element_type=jnp.float32)
    grad_up = lax.dot_general(rows_x, grad_upre, (((0,), (0,)), ((), ())), preferred_element_type=jnp.float32)
    grad_down = lax.dot_general(hidden_bf, scaled_dy, (((0,), (0,)), ((), ())), preferred_element_type=jnp.float32)
    return rows_part, prob_part, grad_gate, grad_up, grad_down


def reference(tokens, grad_out, route_weight, expert_ids, w_gate, w_up, w_down):
    pairs = TOK_DEV * TOP
    total_pairs = N_EXPERT * pairs
    block_ids = expert_ids.reshape(N_EXPERT, pairs)
    flat_ids, position = jax.vmap(lambda ids: slot_positions(ids, EXPERTS))(block_ids)
    source = jnp.broadcast_to(jnp.arange(N_EXPERT, dtype=jnp.int32)[:, None], flat_ids.shape)
    pair_index = source * pairs + jnp.arange(pairs, dtype=jnp.int32)[None, :]
    occupant = jnp.full((EXPERTS, N_EXPERT, CAP), total_pairs, jnp.int32)
    occupant = occupant.at[flat_ids, source, position].set(pair_index)
    gate_full = w_gate.reshape(EXPERTS, SPLIT, D, HID_DEV).transpose(0, 2, 1, 3).reshape(EXPERTS, D, EXP_HID)
    up_full = w_up.reshape(EXPERTS, SPLIT, D, HID_DEV).transpose(0, 2, 1, 3).reshape(EXPERTS, D, EXP_HID)
    down_full = w_down.reshape(EXPERTS, EXP_HID, D)
    flat_weight = route_weight.reshape(-1)

    def per_expert(items):
        taken, gate_mat, up_mat, down_mat = items
        taken = taken.reshape(-1)
        filled = taken < total_pairs
        safe_pair = jnp.minimum(taken, total_pairs - 1)
        token_index = safe_pair // TOP
        rows_x = jnp.where(filled[:, None], tokens[token_index], jnp.zeros((), tokens.dtype))
        rows_dy = jnp.where(filled[:, None], grad_out[token_index], jnp.zeros((), grad_out.dtype))
        rows_weight = jnp.where(filled, flat_weight[safe_pair], jnp.zeros((), route_weight.dtype))
        rows_part, prob_part, grad_gate, grad_up, grad_down = expert_pass(rows_x, rows_dy, rows_weight, gate_mat, up_mat, down_mat)
        grad_rows = jnp.sum(rows_part.astype(jnp.float32), axis=0)
        grad_prob = jnp.sum(prob_part.astype(jnp.float32), axis=1)
        grad_rows = jnp.where(filled[:, None], grad_rows, jnp.zeros((), jnp.float32))
        grad_prob = jnp.where(filled, grad_prob, jnp.zeros((), jnp.float32))
        return grad_rows, grad_prob, grad_gate.astype(jnp.bfloat16), grad_up.astype(jnp.bfloat16), grad_down.astype(jnp.bfloat16), safe_pair

    grad_rows, grad_prob, grad_gate, grad_up, grad_down, safe_pair = lax.map(per_expert, (occupant, gate_full, up_full, down_full))
    safe_pair = safe_pair.reshape(-1)
    grad_tokens = jnp.zeros((TOKENS, D), jnp.float32).at[safe_pair // TOP].add(grad_rows.reshape(-1, D))
    grad_combine = jnp.zeros((total_pairs,), jnp.float32).at[safe_pair].add(grad_prob.reshape(-1))
    grad_gate = grad_gate.reshape(EXPERTS, D, SPLIT, HID_DEV).transpose(0, 2, 1, 3).reshape(EXPERTS * SPLIT, D, HID_DEV)
    grad_up = grad_up.reshape(EXPERTS, D, SPLIT, HID_DEV).transpose(0, 2, 1, 3).reshape(EXPERTS * SPLIT, D, HID_DEV)
    grad_down = grad_down.reshape(EXPERTS * SPLIT, HID_DEV, D)
    return (grad_tokens.astype(jnp.bfloat16), grad_combine.reshape(TOKENS, TOP), grad_gate, grad_up, grad_down)
```

```python
import jax
import jax.numpy as jnp
from jax import lax
from jax.sharding import PartitionSpec as P

SPLIT = 8
CORE = 1
WEIGHT_BIT = 2
ROW_BIT = 4

F32 = jnp.float32
BF16 = jnp.bfloat16


def dot(a, b, ca, cb):
    return lax.dot_general(a, b, (((ca,), (cb,)), ((), ())), preferred_element_type=F32)


def flip(x, mask):
    n = lax.axis_size("expert")
    return lax.ppermute(x, "expert", [(i, i ^ mask) for i in range(n)])


def add(a, b):
    return (a.astype(F32) + b.astype(F32)).astype(BF16)


def share_rows(a):
    pair = jnp.concatenate([a, flip(a, ROW_BIT)], axis=0)
    return jnp.concatenate([pair, flip(pair, CORE)], axis=0)


def sum_rows(p):
    half = p.shape[0] // 2
    p = add(p[:half], flip(p[half:], CORE))
    half = half // 2
    return add(p[:half], flip(p[half:], ROW_BIT))


def on_device(tokens, grad_out, route_weight, expert_ids, w_gate, w_up, w_down):
    axis_count = lax.axis_size("expert")
    experts = axis_count // SPLIT
    tok_rows, features = tokens.shape
    capacity = min(tok_rows, 5 * tok_rows // (4 * experts))
    hid = w_gate.shape[2]
    mine = lax.axis_index("expert") // SPLIT

    relative = expert_ids[:, 0] ^ mine
    onehot = (relative[:, None] == jnp.arange(experts, dtype=jnp.int32)[None, :]).astype(BF16)
    earlier = (jnp.arange(tok_rows)[:, None] > jnp.arange(tok_rows)[None, :]).astype(BF16)
    before = dot(earlier, onehot, 1, 0)
    position = jnp.sum(before * onehot.astype(F32), axis=1).astype(jnp.int32)
    slot = relative * capacity + position
    select = (jnp.arange(experts * capacity, dtype=jnp.int32)[:, None] == slot[None, :]).astype(BF16)

    weight = route_weight.astype(F32)
    scaled = (weight * grad_out.astype(F32)).astype(BF16)
    slots_x = dot(select, tokens, 1, 0).astype(BF16)
    slots_u = dot(select, scaled, 1, 0).astype(BF16)

    def dispatch(slots):
        parts = [
            flip(slots[k * capacity : (k + 1) * capacity], SPLIT * k) for k in range(1, experts)
        ]
        return parts[0] if experts == 2 else jnp.concatenate(parts, axis=0)

    far_x = dispatch(slots_x)
    far_u = dispatch(slots_u)
    near_x = share_rows(slots_x[:capacity])
    near_u = share_rows(slots_u[:capacity])
    far_x = share_rows(far_x)
    far_u = share_rows(far_u)

    gate = w_gate[0]
    up = w_up[0]
    down = w_down[0]
    gate = jnp.concatenate([gate, flip(gate, WEIGHT_BIT)], axis=1)
    up = jnp.concatenate([up, flip(up, WEIGHT_BIT)], axis=1)
    down = jnp.concatenate([down, flip(down, WEIGHT_BIT)], axis=0)

    def hidden_pass(x, u):
        gate_pre = dot(x, gate, 1, 0)
        up_pre = dot(x, up, 1, 0)
        grad_act = dot(u, down, 1, 1)
        sigma = jax.nn.sigmoid(gate_pre)
        act_silu = gate_pre * sigma
        hidden = act_silu * up_pre
        prob = jnp.sum(hidden * grad_act, axis=1, keepdims=True).astype(BF16)
        grad_gpre = (grad_act * up_pre * sigma * (1.0 + gate_pre * (1.0 - sigma))).astype(BF16)
        grad_upre = (grad_act * act_silu).astype(BF16)
        return hidden.astype(BF16), grad_gpre, grad_upre, prob

    def rows_pass(grad_gpre, grad_upre, prob):
        rows = (dot(grad_gpre, gate, 1, 1) + dot(grad_upre, up, 1, 1)).astype(BF16)
        return jnp.concatenate([rows, jnp.broadcast_to(prob, (rows.shape[0], 128))], axis=1)

    near = hidden_pass(near_x, near_u)
    far = hidden_pass(far_x, far_u)
    far_rows = sum_rows(rows_pass(*far[1:]))
    near_rows = sum_rows(rows_pass(*near[1:]))
    back = [
        flip(far_rows[(k - 1) * capacity : k * capacity], SPLIT * k) for k in range(1, experts)
    ]
    slot_rows = jnp.concatenate([near_rows] + back, axis=0)

    x = jnp.concatenate([near_x, far_x], axis=0)
    u = jnp.concatenate([near_u, far_u], axis=0)
    hidden, grad_gpre, grad_upre = (
        jnp.concatenate([a, b], axis=0) for a, b in zip(near[:3], far[:3])
    )

    def weight_grad(a, b, swap):
        if swap:
            far_part = dot(b[:, hid:], a, 0, 0).astype(BF16)
            near_part = dot(b[:, :hid], a, 0, 0)
        else:
            far_part = dot(a, b[:, hid:], 0, 0).astype(BF16)
            near_part = dot(a, b[:, :hid], 0, 0)
        return (near_part + flip(far_part, WEIGHT_BIT).astype(F32)).astype(BF16)[None]

    grad_down = weight_grad(u, hidden, True)
    grad_gate = weight_grad(x, grad_gpre, False)
    grad_up = weight_grad(x, grad_upre, False)

    out = dot(select, slot_rows, 0, 0)
    grad_tokens = out[:, :features].astype(BF16)
    grad_combine = out[:, features : features + 1] / weight
    return (grad_tokens, grad_combine, grad_gate, grad_up, grad_down)


def solution(mesh):
    rows = P(("groups", "expert"), None)
    blocks = P(("groups", "expert"), None, None)
    weights = P("expert", None, None)
    return jax.shard_map(
        on_device,
        mesh=mesh,
        in_specs=(rows, rows, rows, rows, weights, weights, weights),
        out_specs=(rows, rows, blocks, blocks, blocks),
        check_vma=False,
    )
```

```python
import jax
import jax.numpy as jnp
from jax import lax
from jax.sharding import PartitionSpec as P

SPLIT = 8
CORE = 1
WEIGHT_BIT = 2
ROW_BIT = 4

F32 = jnp.float32
BF16 = jnp.bfloat16


def dot(a, b, ca, cb):
    return lax.dot_general(a, b, (((ca,), (cb,)), ((), ())), preferred_element_type=F32)


def flip(x, mask):
    n = lax.axis_size("expert")
    return lax.ppermute(x, "expert", [(i, i ^ mask) for i in range(n)])


def add(a, b):
    return (a.astype(F32) + b.astype(F32)).astype(BF16)


def share_rows(a):
    pair = jnp.concatenate([a, flip(a, ROW_BIT)], axis=0)
    return jnp.concatenate([pair, flip(pair, CORE)], axis=0)


def sum_rows(p):
    half = p.shape[0] // 2
    p = add(p[:half], flip(p[half:], CORE))
    half = half // 2
    return add(p[:half], flip(p[half:], ROW_BIT))


def on_device(tokens, grad_out, route_weight, expert_ids, w_gate, w_up, w_down):
    axis_count = lax.axis_size("expert")
    experts = axis_count // SPLIT
    tok_rows, features = tokens.shape
    capacity = min(tok_rows, 5 * tok_rows // (4 * experts))
    hid = w_gate.shape[2]
    mine = lax.axis_index("expert") // SPLIT

    relative = expert_ids[:, 0] ^ mine
    onehot = (relative[:, None] == jnp.arange(experts, dtype=jnp.int32)[None, :]).astype(BF16)
    earlier = (jnp.arange(tok_rows)[:, None] > jnp.arange(tok_rows)[None, :]).astype(BF16)
    before = dot(earlier, onehot, 1, 0)
    position = jnp.sum(before * onehot.astype(F32), axis=1).astype(jnp.int32)
    slot = relative * capacity + position
    select = (jnp.arange(experts * capacity, dtype=jnp.int32)[:, None] == slot[None, :]).astype(BF16)

    weight = route_weight.astype(F32)
    scaled = (weight * grad_out.astype(F32)).astype(BF16)
    slots_x = dot(select, tokens, 1, 0).astype(BF16)
    slots_u = dot(select, scaled, 1, 0).astype(BF16)

    def dispatch(slots):
        parts = [
            flip(slots[k * capacity : (k + 1) * capacity], SPLIT * k) for k in range(1, experts)
        ]
        return parts[0] if experts == 2 else jnp.concatenate(parts, axis=0)

    far_x = dispatch(slots_x)
    near = share_rows(jnp.concatenate([slots_x[:capacity], slots_u[:capacity]], axis=1))
    far_u = dispatch(slots_u)
    near_x, near_u = near[:, :features], near[:, features:]
    far_x = share_rows(far_x)
    far_u = share_rows(far_u)

    gate, up, down = w_gate[0], w_up[0], w_down[0]
    other = flip(jnp.concatenate([gate, up, down.reshape(features, hid)], axis=0), WEIGHT_BIT)
    gate = jnp.concatenate([gate, other[:features]], axis=1)
    up = jnp.concatenate([up, other[features : 2 * features]], axis=1)
    down = jnp.concatenate([down, other[2 * features :].reshape(hid, features)], axis=0)

    def hidden_pass(x, u):
        gate_pre = dot(x, gate, 1, 0)
        up_pre = dot(x, up, 1, 0)
        grad_act = dot(u, down, 1, 1)
        sigma = jax.nn.sigmoid(gate_pre)
        act_silu = gate_pre * sigma
        hidden = act_silu * up_pre
        prob = jnp.sum(hidden * grad_act, axis=1, keepdims=True).astype(BF16)
        grad_gpre = (grad_act * up_pre * sigma * (1.0 + gate_pre * (1.0 - sigma))).astype(BF16)
        grad_upre = (grad_act * act_silu).astype(BF16)
        return hidden.astype(BF16), grad_gpre, grad_upre, prob

    def rows_pass(grad_gpre, grad_upre, prob):
        rows = (dot(grad_gpre, gate, 1, 1) + dot(grad_upre, up, 1, 1)).astype(BF16)
        return jnp.concatenate([rows, jnp.broadcast_to(prob, (rows.shape[0], 128))], axis=1)

    near = hidden_pass(near_x, near_u)
    far = hidden_pass(far_x, far_u)
    far_rows = sum_rows(rows_pass(*far[1:]))
    near_rows = sum_rows(rows_pass(*near[1:]))
    back = [
        flip(far_rows[(k - 1) * capacity : k * capacity], SPLIT * k) for k in range(1, experts)
    ]

    x = jnp.concatenate([near_x, far_x], axis=0)
    u = jnp.concatenate([near_u, far_u], axis=0)
    hidden, grad_gpre, grad_upre = (
        jnp.concatenate([a, b], axis=0) for a, b in zip(near[:3], far[:3])
    )
    theirs = jnp.concatenate([grad_gpre[:, hid:], grad_upre[:, hid:]], axis=1)
    ours = jnp.concatenate([grad_gpre[:, :hid], grad_upre[:, :hid]], axis=1)
    got_both = flip(dot(x, theirs, 0, 0).astype(BF16), WEIGHT_BIT)
    got_down = flip(dot(hidden[:, hid:], u, 0, 0).astype(BF16), WEIGHT_BIT)
    near_rows, back, got_both, got_down = lax.optimization_barrier(
        (near_rows, back, got_both, got_down)
    )
    both = (dot(x, ours, 0, 0) + got_both.astype(F32)).astype(BF16)
    grad_gate = both[:, :hid][None]
    grad_up = both[:, hid:][None]
    grad_down = (dot(hidden[:, :hid], u, 0, 0) + got_down.astype(F32)).astype(BF16)[None]
    slot_rows = jnp.concatenate([near_rows] + back, axis=0)

    out = dot(select, slot_rows, 0, 0)
    grad_tokens = out[:, :features].astype(BF16)
    grad_combine = out[:, features : features + 1] / weight
    return (grad_tokens, grad_combine, grad_gate, grad_up, grad_down)


def solution(mesh):
    rows = P(("groups", "expert"), None)
    blocks = P(("groups", "expert"), None, None)
    weights = P("expert", None, None)
    return jax.shard_map(
        on_device,
        mesh=mesh,
        in_specs=(rows, rows, rows, rows, weights, weights, weights),
        out_specs=(rows, rows, blocks, blocks, blocks),
        check_vma=False,
    )
```

```python
import jax
import jax.numpy as jnp
from jax import lax
from jax.sharding import PartitionSpec as P

SPLIT = 8
CORE = 1
WEIGHT_BIT = 2
ROW_BIT = 4

F32 = jnp.float32
BF16 = jnp.bfloat16


def dot(a, b, ca, cb):
    return lax.dot_general(a, b, (((ca,), (cb,)), ((), ())), preferred_element_type=F32)


def flip(x, mask):
    n = lax.axis_size("expert")
    return lax.ppermute(x, "expert", [(i, i ^ mask) for i in range(n)])


def add(a, b):
    return (a.astype(F32) + b.astype(F32)).astype(BF16)


def after(x, *others):
    return lax.optimization_barrier((x,) + others)[0]


def share_core(a, b):
    pair = jnp.concatenate([a, b], axis=0)
    return jnp.concatenate([pair, flip(pair, CORE)], axis=0)


def sum_rows(p):
    half = p.shape[0] // 2
    p = add(p[:half], flip(p[half:], CORE))
    half = half // 2
    return add(p[:half], flip(p[half:], ROW_BIT))


def on_device(tokens, grad_out, route_weight, expert_ids, w_gate, w_up, w_down):
    axis_count = lax.axis_size("expert")
    experts = axis_count // SPLIT
    tok_rows, features = tokens.shape
    hid = w_gate.shape[2]
    capacity = min(tok_rows, 5 * tok_rows // (4 * experts))
    capacity = -(-capacity // 16) * 16
    mine = lax.axis_index("expert") // SPLIT

    relative = expert_ids[:, 0] ^ mine
    onehot = (relative[:, None] == jnp.arange(experts, dtype=jnp.int32)[None, :]).astype(BF16)
    earlier = (jnp.arange(tok_rows)[:, None] > jnp.arange(tok_rows)[None, :]).astype(BF16)
    before = dot(earlier, onehot, 1, 0)
    position = jnp.sum(before * onehot.astype(F32), axis=1).astype(jnp.int32)
    slot = relative * capacity + position
    select = (jnp.arange(experts * capacity, dtype=jnp.int32)[:, None] == slot[None, :]).astype(BF16)

    weight = route_weight.astype(F32)
    scaled = (weight * grad_out.astype(F32)).astype(BF16)

    def pick(source):
        parts = [select[k * capacity : (k + 1) * capacity] for k in range(experts)]
        return [dot(part, source, 1, 0).astype(BF16) for part in parts]

    def dispatch(parts):
        got = [flip(part, SPLIT * k) for k, part in enumerate(parts, 1)]
        return got[0] if experts == 2 else jnp.concatenate(got, axis=0)

    near_x, *far_x = pick(tokens)
    near_u, *far_u = pick(scaled)
    gate, up, down = w_gate[0], w_up[0], w_down[0]
    gate_b, up_b = flip(gate, WEIGHT_BIT), flip(up, WEIGHT_BIT)

    far_x = dispatch(far_x)
    near_x2 = flip(near_x, ROW_BIT)
    far_x, near_x2, near_u, down_send, *far_u = lax.optimization_barrier(
        (far_x, near_x2, near_u, down, *far_u)
    )
    far_u = dispatch(far_u)
    far_x2 = flip(far_x, ROW_BIT)
    down_b = flip(down_send, WEIGHT_BIT)
    far_u, gate_b, up_b = lax.optimization_barrier((far_u, gate_b, up_b))
    far_u2 = flip(far_u, ROW_BIT)
    near_u, down_b, far_u2 = lax.optimization_barrier((near_u, down_b, far_u2))
    near_u2 = flip(near_u, ROW_BIT)

    far_x = share_core(far_x, far_x2)
    far_u = share_core(far_u, far_u2)
    near_x = share_core(near_x, near_x2)

    gate = jnp.concatenate([gate, gate_b], axis=1)
    up = jnp.concatenate([up, up_b], axis=1)
    down = jnp.concatenate([down, down_b], axis=0)

    def hidden_pass(x, u):
        gate_pre = dot(x, gate, 1, 0)
        up_pre = dot(x, up, 1, 0)
        grad_act = dot(u, down, 1, 1)
        sigma = jax.nn.sigmoid(gate_pre)
        act_silu = gate_pre * sigma
        hidden = act_silu * up_pre
        prob = jnp.sum(hidden * grad_act, axis=1, keepdims=True).astype(BF16)
        grad_gpre = (grad_act * up_pre * sigma * (1.0 + gate_pre * (1.0 - sigma))).astype(BF16)
        grad_upre = (grad_act * act_silu).astype(BF16)
        return hidden.astype(BF16), grad_gpre, grad_upre, prob

    def rows_pass(grad_gpre, grad_upre, prob):
        rows = (dot(grad_gpre, gate, 1, 1) + dot(grad_upre, up, 1, 1)).astype(BF16)
        return jnp.concatenate([rows, jnp.broadcast_to(prob, (rows.shape[0], 128))], axis=1)

    far = hidden_pass(far_x, far_u)
    far_rows, near_u2 = lax.optimization_barrier((rows_pass(*far[1:]), near_u2))
    near_u = share_core(near_u, near_u2)
    far_rows = sum_rows(far_rows)
    back = [
        flip(far_rows[(k - 1) * capacity : k * capacity], SPLIT * k) for k in range(1, experts)
    ]
    near = hidden_pass(near_x, near_u)
    near_rows = sum_rows(rows_pass(*near[1:]))

    x = jnp.concatenate([near_x, far_x], axis=0)
    u = jnp.concatenate([near_u, far_u], axis=0)
    hidden, grad_gpre, grad_upre = (
        jnp.concatenate([a, b], axis=0) for a, b in zip(near[:3], far[:3])
    )
    def weight_grads(at):
        return (
            dot(x, grad_gpre[:, at], 0, 0), dot(x, grad_upre[:, at], 0, 0), dot(hidden[:, at], u, 0, 0)
        )

    got = [flip(g.astype(BF16), WEIGHT_BIT) for g in weight_grads(slice(hid, None))]
    kept = lax.optimization_barrier(weight_grads(slice(0, hid)))
    near_rows, back, got, kept = lax.optimization_barrier((near_rows, back, got, kept))
    grad_gate, grad_up, grad_down = (
        (a + b.astype(F32)).astype(BF16)[None] for a, b in zip(kept, got)
    )
    slot_rows = jnp.concatenate([near_rows] + back, axis=0)
    out = dot(select, slot_rows, 0, 0)
    grad_tokens = out[:, :features].astype(BF16)
    grad_combine = out[:, features : features + 1] / weight
    return (grad_tokens, grad_combine, grad_gate, grad_up, grad_down)


def solution(mesh):
    rows = P(("groups", "expert"), None)
    blocks = P(("groups", "expert"), None, None)
    weights = P("expert", None, None)
    return jax.shard_map(
        on_device,
        mesh=mesh,
        in_specs=(rows, rows, rows, rows, weights, weights, weights),
        out_specs=(rows, rows, blocks, blocks, blocks),
        check_vma=False,
    )
```

```python
import jax
import jax.numpy as jnp
from jax import lax
from jax.sharding import PartitionSpec as P

SPLIT = 8
CORE = 1
WEIGHT_BIT = 2
ROW_BIT = 4

F32 = jnp.float32
BF16 = jnp.bfloat16


def dot(a, b, ca, cb):
    return lax.dot_general(a, b, (((ca,), (cb,)), ((), ())), preferred_element_type=F32)


def flip(x, mask):
    n = lax.axis_size("expert")
    return lax.ppermute(x, "expert", [(i, i ^ mask) for i in range(n)])


def add(a, b):
    return (a.astype(F32) + b.astype(F32)).astype(BF16)


def after(x, *others):
    return lax.optimization_barrier((x,) + others)[0]


def share_core(a, b):
    pair = jnp.concatenate([a, b], axis=0)
    return jnp.concatenate([pair, flip(pair, CORE)], axis=0)


def sum_rows(p):
    half = p.shape[0] // 2
    p = add(p[:half], flip(p[half:], CORE))
    half = half // 2
    return add(p[:half], flip(p[half:], ROW_BIT))


def on_device(tokens, grad_out, route_weight, expert_ids, w_gate, w_up, w_down):
    axis_count = lax.axis_size("expert")
    experts = axis_count // SPLIT
    tok_rows, features = tokens.shape
    hid = w_gate.shape[2]
    capacity = min(tok_rows, 5 * tok_rows // (4 * experts))
    capacity = -(-capacity // 16) * 16
    mine = lax.axis_index("expert") // SPLIT

    relative = expert_ids[:, 0] ^ mine
    onehot = (relative[:, None] == jnp.arange(experts, dtype=jnp.int32)[None, :]).astype(BF16)
    earlier = (jnp.arange(tok_rows)[:, None] > jnp.arange(tok_rows)[None, :]).astype(BF16)
    before = dot(earlier, onehot, 1, 0)
    position = jnp.sum(before * onehot.astype(F32), axis=1).astype(jnp.int32)
    slot = relative * capacity + position
    select = (jnp.arange(experts * capacity, dtype=jnp.int32)[:, None] == slot[None, :]).astype(BF16)

    weight = route_weight.astype(F32)
    scaled = (weight * grad_out.astype(F32)).astype(BF16)

    def pick(source):
        parts = [select[k * capacity : (k + 1) * capacity] for k in range(experts)]
        return [dot(part, source, 1, 0).astype(BF16) for part in parts]

    def dispatch(parts):
        got = [flip(part, SPLIT * k) for k, part in enumerate(parts, 1)]
        return got[0] if experts == 2 else jnp.concatenate(got, axis=0)

    near_x, *far_x = pick(tokens)
    near_u, *far_u = pick(scaled)
    gate, up, down = w_gate[0], w_up[0], w_down[0]
    gate_b, up_b = flip(gate, WEIGHT_BIT), flip(up, WEIGHT_BIT)

    far_x = dispatch(far_x)
    near_x2 = flip(near_x, ROW_BIT)
    far_x, near_x2, near_u, down_send, *far_u = lax.optimization_barrier(
        (far_x, near_x2, near_u, down, *far_u)
    )
    far_u = dispatch(far_u)
    far_x2 = flip(far_x, ROW_BIT)
    down_b = flip(down_send, WEIGHT_BIT)
    far_u, gate_b, up_b = lax.optimization_barrier((far_u, gate_b, up_b))
    far_u2 = flip(far_u, ROW_BIT)
    near_u, down_b, far_u2 = lax.optimization_barrier((near_u, down_b, far_u2))
    near_u2 = flip(near_u, ROW_BIT)

    far_x = share_core(far_x, far_x2)
    far_u = share_core(far_u, far_u2)
    near_x = share_core(near_x, near_x2)

    gate = jnp.concatenate([gate, gate_b], axis=1)
    up = jnp.concatenate([up, up_b], axis=1)
    down = jnp.concatenate([down, down_b], axis=0)

    def hidden_pass(x, u):
        gate_pre = dot(x, gate, 1, 0)
        up_pre = dot(x, up, 1, 0)
        grad_act = dot(u, down, 1, 1)
        sigma = jax.nn.sigmoid(gate_pre)
        act_silu = gate_pre * sigma
        hidden = act_silu * up_pre
        prob = jnp.sum(hidden * grad_act, axis=1, keepdims=True).astype(BF16)
        grad_gpre = (grad_act * up_pre * sigma * (1.0 + gate_pre * (1.0 - sigma))).astype(BF16)
        grad_upre = (grad_act * act_silu).astype(BF16)
        return hidden.astype(BF16), grad_gpre, grad_upre, prob

    def rows_pass(grad_gpre, grad_upre, prob):
        rows = (dot(grad_gpre, gate, 1, 1) + dot(grad_upre, up, 1, 1)).astype(BF16)
        return jnp.concatenate([rows, jnp.broadcast_to(prob, (rows.shape[0], 128))], axis=1)

    far = hidden_pass(far_x, far_u)
    far_rows, near_u2 = lax.optimization_barrier((rows_pass(*far[1:]), near_u2))
    near_u = share_core(near_u, near_u2)
    far_rows = sum_rows(far_rows)
    back = [
        flip(far_rows[(k - 1) * capacity : k * capacity], SPLIT * k) for k in range(1, experts)
    ]
    near = hidden_pass(near_x, near_u)
    near_rows = sum_rows(rows_pass(*near[1:]))

    x = jnp.concatenate([near_x, far_x], axis=0)
    u = jnp.concatenate([near_u, far_u], axis=0)
    hidden, grad_gpre, grad_upre = (
        jnp.concatenate([a, b], axis=0) for a, b in zip(near[:3], far[:3])
    )
    def weight_grads(at):
        return (
            dot(x, grad_gpre[:, at], 0, 0), dot(x, grad_upre[:, at], 0, 0), dot(hidden[:, at], u, 0, 0)
        )

    got = [flip(g.astype(BF16), WEIGHT_BIT) for g in weight_grads(slice(hid, None))]
    slot_rows = jnp.concatenate([near_rows] + back, axis=0)
    out = dot(select, slot_rows, 0, 0)
    grad_tokens = out[:, :features].astype(BF16)
    grad_combine = out[:, features : features + 1] / weight

    grads = []
    before = grad_tokens
    for own, other in zip(weight_grads(slice(0, hid)), got):
        other, before = lax.optimization_barrier((other, before))
        if not grads:
            grad_tokens = before
        else:
            grads[-1] = before
        before = (own + other.astype(F32)).astype(BF16)
        grads.append(before)
    grad_gate, grad_up, grad_down = (g[None] for g in grads)
    return (grad_tokens, grad_combine, grad_gate, grad_up, grad_down)


def solution(mesh):
    rows = P(("groups", "expert"), None)
    blocks = P(("groups", "expert"), None, None)
    weights = P("expert", None, None)
    return jax.shard_map(
        on_device,
        mesh=mesh,
        in_specs=(rows, rows, rows, rows, weights, weights, weights),
        out_specs=(rows, rows, blocks, blocks, blocks),
        check_vma=False,
    )
```

```python
import jax
import jax.numpy as jnp
from jax import lax
from jax.sharding import PartitionSpec as P

SPLIT = 8
CORE = 1
WEIGHT_BIT = 2
ROW_BIT = 4
SHARED_PART = 3

F32 = jnp.float32
BF16 = jnp.bfloat16


def dot(a, b, ca, cb):
    return lax.dot_general(a, b, (((ca,), (cb,)), ((), ())), preferred_element_type=F32)


def flip(x, mask):
    n = lax.axis_size("expert")
    return lax.ppermute(x, "expert", [(i, i ^ mask) for i in range(n)])


def add(a, b):
    return (a.astype(F32) + b.astype(F32)).astype(BF16)


def after(x, *others):
    return lax.optimization_barrier((x,) + others)[0]


def share_core(pair):
    return jnp.concatenate([pair, flip(pair, CORE)], axis=0)


def sum_rows(p):
    half = p.shape[0] // 2
    p = add(p[:half], flip(p[half:], CORE))
    half = half // 2
    return add(p[:half], flip(p[half:], ROW_BIT))


def on_device(tokens, grad_out, route_weight, expert_ids, w_gate, w_up, w_down):
    axis_count = lax.axis_size("expert")
    experts = axis_count // SPLIT
    tok_rows, features = tokens.shape
    hid = w_gate.shape[2]
    shared = features * SHARED_PART // 7 // 128 * 128
    capacity = min(tok_rows, 5 * tok_rows // (4 * experts))
    capacity = -(-capacity // 16) * 16
    mine = lax.axis_index("expert") // SPLIT

    relative = expert_ids[:, 0] ^ mine
    onehot = (relative[:, None] == jnp.arange(experts, dtype=jnp.int32)[None, :]).astype(BF16)
    earlier = (jnp.arange(tok_rows)[:, None] > jnp.arange(tok_rows)[None, :]).astype(BF16)
    before = dot(earlier, onehot, 1, 0)
    position = jnp.sum(before * onehot.astype(F32), axis=1).astype(jnp.int32)
    slot = relative * capacity + position
    select = (jnp.arange(experts * capacity, dtype=jnp.int32)[:, None] == slot[None, :]).astype(BF16)

    weight = route_weight.astype(F32)
    scaled = (weight * grad_out.astype(F32)).astype(BF16)

    def pick(source):
        parts = [select[k * capacity : (k + 1) * capacity] for k in range(experts)]
        return [dot(part, source, 1, 0).astype(BF16) for part in parts]

    def dispatch(parts):
        got = [flip(part, SPLIT * k) for k, part in enumerate(parts, 1)]
        return got[0] if experts == 2 else jnp.concatenate(got, axis=0)

    near_x, *far_x = pick(tokens)
    near_u, *far_u = pick(scaled)
    gate, up, down = w_gate[0], w_up[0], w_down[0]
    gate_b, up_b = flip(gate, WEIGHT_BIT), flip(up, WEIGHT_BIT)

    far_x = dispatch(far_x)
    near_x2 = flip(near_x, ROW_BIT)
    far_x, near_x2, near_u, gate_b, *far_u = lax.optimization_barrier(
        (far_x, near_x2, near_u, gate_b, *far_u)
    )
    up_b, down_send = lax.optimization_barrier((up_b, down))
    far_u = dispatch(far_u)
    far_x2 = flip(far_x, ROW_BIT)
    down_b = flip(down_send, WEIGHT_BIT)
    near_x = jnp.concatenate([near_x, near_x2], axis=0)
    far_x2, near_p = lax.optimization_barrier((far_x2, near_x[:, :shared]))
    near_p = flip(near_p, WEIGHT_BIT)
    far_u2 = flip(far_u, ROW_BIT)
    far_x = jnp.concatenate([far_x, far_x2], axis=0)
    near_u, down_b, far_u2, near_p, far_p = lax.optimization_barrier(
        (near_u, down_b, far_u2, near_p, far_x[:, :shared])
    )
    far_p = flip(far_p, WEIGHT_BIT)
    near_u2 = flip(near_u, ROW_BIT)

    far_x = share_core(far_x)
    far_u = share_core(jnp.concatenate([far_u, far_u2], axis=0))
    near_x = share_core(near_x)

    gate = jnp.concatenate([gate, gate_b], axis=1)
    up = jnp.concatenate([up, up_b], axis=1)
    down = jnp.concatenate([down, down_b], axis=0)

    def hidden_pass(x, u):
        gate_pre = dot(x, gate, 1, 0)
        up_pre = dot(x, up, 1, 0)
        grad_act = dot(u, down, 1, 1)
        sigma = jax.nn.sigmoid(gate_pre)
        act_silu = gate_pre * sigma
        hidden = act_silu * up_pre
        prob = jnp.sum(hidden * grad_act, axis=1, keepdims=True).astype(BF16)
        grad_gpre = (grad_act * up_pre * sigma * (1.0 + gate_pre * (1.0 - sigma))).astype(BF16)
        grad_upre = (grad_act * act_silu).astype(BF16)
        return hidden.astype(BF16), grad_gpre, grad_upre, prob

    def rows_pass(grad_gpre, grad_upre, prob):
        rows = (dot(grad_gpre, gate, 1, 1) + dot(grad_upre, up, 1, 1)).astype(BF16)
        return jnp.concatenate([rows, jnp.broadcast_to(prob, (rows.shape[0], 128))], axis=1)

    far = hidden_pass(far_x, far_u)
    far_rows, near_u2, far_p = lax.optimization_barrier((rows_pass(*far[1:]), near_u2, far_p))
    near_u = share_core(jnp.concatenate([near_u, near_u2], axis=0))
    far_rows = sum_rows(far_rows)
    back = [
        flip(far_rows[(k - 1) * capacity : k * capacity], SPLIT * k) for k in range(1, experts)
    ]
    near = hidden_pass(near_x, near_u)
    near_rows = sum_rows(rows_pass(*near[1:]))

    x = jnp.concatenate([near_x, far_x], axis=0)
    u = jnp.concatenate([near_u, far_u], axis=0)
    hidden, grad_gpre, grad_upre = (
        jnp.concatenate([a, b], axis=0) for a, b in zip(near[:3], far[:3])
    )
    both = jnp.concatenate([grad_gpre[:, :hid], grad_upre[:, :hid]], axis=1)
    both_p = jnp.concatenate([grad_gpre[:, hid:], grad_upre[:, hid:]], axis=1)
    got_both = flip(both_p, WEIGHT_BIT)
    rest_p = dot(x[:, shared:], both_p, 0, 0).astype(BF16)
    down_p = dot(hidden[:, hid:], u, 0, 0).astype(BF16)
    x_p = jnp.concatenate([near_p, far_p], axis=0)
    rest_p, down_p, x_p = lax.optimization_barrier((rest_p, down_p, x_p))
    x_p_core = flip(x_p, CORE)
    at = x_p.shape[0] // 2
    x_p = jnp.concatenate([x_p[:at], x_p_core[:at], x_p[at:], x_p_core[at:]], axis=0)
    got_rest = flip(rest_p, WEIGHT_BIT)
    got_down = flip(down_p, WEIGHT_BIT)

    slot_rows = jnp.concatenate([near_rows] + back, axis=0)
    out = dot(select, slot_rows, 0, 0)
    grad_tokens = out[:, :features].astype(BF16)
    grad_combine = out[:, features : features + 1] / weight

    first = (dot(x[:, :shared], both, 0, 0) + dot(x_p, got_both, 0, 0)).astype(BF16)
    got_rest, first, grad_tokens = lax.optimization_barrier((got_rest, first, grad_tokens))
    rest = (dot(x[:, shared:], both, 0, 0) + got_rest.astype(F32)).astype(BF16)
    grad_gate, grad_up = (
        jnp.concatenate([first[:, at], rest[:, at]], axis=0)[None]
        for at in (slice(0, hid), slice(hid, None))
    )
    got_down, grad_gate, grad_up, grad_combine = lax.optimization_barrier(
        (got_down, grad_gate, grad_up, grad_combine)
    )
    grad_down = (dot(hidden[:, :hid], u, 0, 0) + got_down.astype(F32)).astype(BF16)[None]
    return (grad_tokens, grad_combine, grad_gate, grad_up, grad_down)


def solution(mesh):
    rows = P(("groups", "expert"), None)
    blocks = P(("groups", "expert"), None, None)
    weights = P("expert", None, None)
    return jax.shard_map(
        on_device,
        mesh=mesh,
        in_specs=(rows, rows, rows, rows, weights, weights, weights),
        out_specs=(rows, rows, blocks, blocks, blocks),
        check_vma=False,
    )
```

```python
import jax
import jax.numpy as jnp
from jax import lax
from jax.sharding import PartitionSpec as P

SPLIT = 8
CORE = 1
WEIGHT_BIT = 2
ROW_BIT = 4
SHARED_PART = 3

F32 = jnp.float32
BF16 = jnp.bfloat16


def dot(a, b, ca, cb):
    return lax.dot_general(a, b, (((ca,), (cb,)), ((), ())), preferred_element_type=F32)


def flip(x, mask):
    n = lax.axis_size("expert")
    return lax.ppermute(x, "expert", [(i, i ^ mask) for i in range(n)])


def add(a, b):
    return (a.astype(F32) + b.astype(F32)).astype(BF16)


def after(x, *others):
    return lax.optimization_barrier((x,) + others)[0]


def share_core(pair):
    return jnp.concatenate([pair, flip(pair, CORE)], axis=0)


def sum_rows(p):
    half = p.shape[0] // 2
    p = add(p[:half], flip(p[half:], CORE))
    half = half // 2
    return add(p[:half], flip(p[half:], ROW_BIT))


def on_device(tokens, grad_out, route_weight, expert_ids, w_gate, w_up, w_down):
    axis_count = lax.axis_size("expert")
    experts = axis_count // SPLIT
    tok_rows, features = tokens.shape
    hid = w_gate.shape[2]
    shared = features * SHARED_PART // 7 // 128 * 128
    capacity = min(tok_rows, 5 * tok_rows // (4 * experts))
    capacity = -(-capacity // 16) * 16
    mine = lax.axis_index("expert") // SPLIT

    relative = expert_ids[:, 0] ^ mine
    onehot = (relative[:, None] == jnp.arange(experts, dtype=jnp.int32)[None, :]).astype(BF16)
    earlier = (jnp.arange(tok_rows)[:, None] > jnp.arange(tok_rows)[None, :]).astype(BF16)
    before = dot(earlier, onehot, 1, 0)
    position = jnp.sum(before * onehot.astype(F32), axis=1).astype(jnp.int32)
    slot = relative * capacity + position
    select = (jnp.arange(experts * capacity, dtype=jnp.int32)[:, None] == slot[None, :]).astype(BF16)

    weight = route_weight.astype(F32)
    scaled = (weight * grad_out.astype(F32)).astype(BF16)

    def pick(source):
        parts = [select[k * capacity : (k + 1) * capacity] for k in range(experts)]
        return [dot(part, source, 1, 0).astype(BF16) for part in parts]

    def dispatch(parts):
        got = [flip(part, SPLIT * k) for k, part in enumerate(parts, 1)]
        return got[0] if experts == 2 else jnp.concatenate(got, axis=0)

    near_x, *far_x = pick(tokens)
    near_u, *far_u = pick(scaled)
    gate, up, down = w_gate[0], w_up[0], w_down[0]
    gate_b, up_b = flip(gate, WEIGHT_BIT), flip(up, WEIGHT_BIT)

    far_x = dispatch(far_x)
    near_x2 = flip(near_x, ROW_BIT)
    far_x, near_x2, near_u, gate_b, *far_u = lax.optimization_barrier(
        (far_x, near_x2, near_u, gate_b, *far_u)
    )
    up_b, down_send = lax.optimization_barrier((up_b, down))
    far_u = dispatch(far_u)
    far_x2 = flip(far_x, ROW_BIT)
    down_b = flip(down_send, WEIGHT_BIT)
    near_x = jnp.concatenate([near_x, near_x2], axis=0)
    far_x2, near_p = lax.optimization_barrier((far_x2, near_x[:, :shared]))
    near_p = flip(near_p, WEIGHT_BIT)
    far_u2 = flip(far_u, ROW_BIT)
    far_x = jnp.concatenate([far_x, far_x2], axis=0)
    near_u, down_b, far_u2, near_p, far_p = lax.optimization_barrier(
        (near_u, down_b, far_u2, near_p, far_x[:, :shared])
    )
    far_p = flip(far_p, WEIGHT_BIT)
    near_u2 = flip(near_u, ROW_BIT)

    far_x = share_core(far_x)
    far_u = share_core(jnp.concatenate([far_u, far_u2], axis=0))
    near_x = share_core(near_x)

    gate = jnp.concatenate([gate, gate_b], axis=1)
    up = jnp.concatenate([up, up_b], axis=1)
    down = jnp.concatenate([down, down_b], axis=0)

    def hidden_pass(x, u):
        gate_pre = dot(x, gate, 1, 0)
        up_pre = dot(x, up, 1, 0)
        grad_act = dot(u, down, 1, 1)
        sigma = jax.nn.sigmoid(gate_pre)
        act_silu = gate_pre * sigma
        hidden = act_silu * up_pre
        prob = jnp.sum(hidden * grad_act, axis=1, keepdims=True).astype(BF16)
        grad_gpre = (grad_act * up_pre * sigma * (1.0 + gate_pre * (1.0 - sigma))).astype(BF16)
        grad_upre = (grad_act * act_silu).astype(BF16)
        return hidden.astype(BF16), grad_gpre, grad_upre, prob

    def rows_pass(grad_gpre, grad_upre, prob):
        rows = (dot(grad_gpre, gate, 1, 1) + dot(grad_upre, up, 1, 1)).astype(BF16)
        return jnp.concatenate([rows, jnp.broadcast_to(prob, (rows.shape[0], 128))], axis=1)

    far = hidden_pass(far_x, far_u)
    far_rows, near_u2, far_p = lax.optimization_barrier((rows_pass(*far[1:]), near_u2, far_p))
    near_u = share_core(jnp.concatenate([near_u, near_u2], axis=0))
    far_rows = sum_rows(far_rows)
    back = [
        flip(far_rows[(k - 1) * capacity : k * capacity], SPLIT * k) for k in range(1, experts)
    ]
    near = hidden_pass(near_x, near_u)
    near_rows = sum_rows(rows_pass(*near[1:]))

    x = jnp.concatenate([near_x, far_x], axis=0)
    u = jnp.concatenate([near_u, far_u], axis=0)
    hidden, grad_gpre, grad_upre = (
        jnp.concatenate([a, b], axis=0) for a, b in zip(near[:3], far[:3])
    )
    both = jnp.concatenate([grad_gpre[:, :hid], grad_upre[:, :hid]], axis=1)
    both_p = jnp.concatenate([grad_gpre[:, hid:], grad_upre[:, hid:]], axis=1)
    got_both = flip(both_p, WEIGHT_BIT)
    rest_p = dot(x[:, shared:], both_p, 0, 0).astype(BF16)
    down_p = dot(hidden[:, hid:], u, 0, 0).astype(BF16)
    x_p = jnp.concatenate([near_p, far_p], axis=0)
    rest_p, down_p, x_p = lax.optimization_barrier((rest_p, down_p, x_p))
    x_p_core = flip(x_p, CORE)
    at = x_p.shape[0] // 2
    x_p = jnp.concatenate([x_p[:at], x_p_core[:at], x_p[at:], x_p_core[at:]], axis=0)
    got_rest = flip(rest_p, WEIGHT_BIT)
    got_down = flip(down_p, WEIGHT_BIT)

    slot_rows = jnp.concatenate([near_rows] + back, axis=0)
    out = dot(select, slot_rows, 0, 0)
    grad_tokens = out[:, :features].astype(BF16)
    grad_combine = out[:, features : features + 1] / weight

    first = (dot(x[:, :shared], both, 0, 0) + dot(x_p, got_both, 0, 0)).astype(BF16)
    got_down, first = lax.optimization_barrier((got_down, first))
    grad_down = (dot(hidden[:, :hid], u, 0, 0) + got_down.astype(F32)).astype(BF16)[None]
    got_rest, first, grad_tokens, grad_combine, grad_down = lax.optimization_barrier(
        (got_rest, first, grad_tokens, grad_combine, grad_down)
    )
    rest = (dot(x[:, shared:], both, 0, 0) + got_rest.astype(F32)).astype(BF16)
    grad_gate, grad_up = (
        jnp.concatenate([first[:, at], rest[:, at]], axis=0)[None]
        for at in (slice(0, hid), slice(hid, None))
    )
    return (grad_tokens, grad_combine, grad_gate, grad_up, grad_down)


def solution(mesh):
    rows = P(("groups", "expert"), None)
    blocks = P(("groups", "expert"), None, None)
    weights = P("expert", None, None)
    return jax.shard_map(
        on_device,
        mesh=mesh,
        in_specs=(rows, rows, rows, rows, weights, weights, weights),
        out_specs=(rows, rows, blocks, blocks, blocks),
        check_vma=False,
    )
```

```python
import jax
import jax.numpy as jnp
from jax import lax
from jax.sharding import PartitionSpec as P

SPLIT = 8
CORE = 1
WEIGHT_BIT = 2
ROW_BIT = 4
SHARED_PART = 13

F32 = jnp.float32
BF16 = jnp.bfloat16


def dot(a, b, ca, cb):
    return lax.dot_general(a, b, (((ca,), (cb,)), ((), ())), preferred_element_type=F32)


def flip(x, mask):
    n = lax.axis_size("expert")
    return lax.ppermute(x, "expert", [(i, i ^ mask) for i in range(n)])


def add(a, b):
    return (a.astype(F32) + b.astype(F32)).astype(BF16)


def after(x, *others):
    return lax.optimization_barrier((x,) + others)[0]


def share_core(pair):
    return jnp.concatenate([pair, flip(pair, CORE)], axis=0)


def sum_rows(p):
    half = p.shape[0] // 2
    p = add(p[:half], flip(p[half:], CORE))
    half = half // 2
    return add(p[:half], flip(p[half:], ROW_BIT))


def on_device(tokens, grad_out, route_weight, expert_ids, w_gate, w_up, w_down):
    axis_count = lax.axis_size("expert")
    experts = axis_count // SPLIT
    tok_rows, features = tokens.shape
    hid = w_gate.shape[2]
    shared = features * SHARED_PART // 28 // 128 * 128
    capacity = min(tok_rows, 5 * tok_rows // (4 * experts))
    capacity = -(-capacity // 16) * 16
    mine = lax.axis_index("expert") // SPLIT

    relative = expert_ids[:, 0] ^ mine
    onehot = (relative[:, None] == jnp.arange(experts, dtype=jnp.int32)[None, :]).astype(BF16)
    earlier = (jnp.arange(tok_rows)[:, None] > jnp.arange(tok_rows)[None, :]).astype(BF16)
    before = dot(earlier, onehot, 1, 0)
    position = jnp.sum(before * onehot.astype(F32), axis=1).astype(jnp.int32)
    slot = relative * capacity + position
    select = (jnp.arange(experts * capacity, dtype=jnp.int32)[:, None] == slot[None, :]).astype(BF16)

    weight = route_weight.astype(F32)
    scaled = (weight * grad_out.astype(F32)).astype(BF16)

    def pick(source):
        parts = [select[k * capacity : (k + 1) * capacity] for k in range(experts)]
        return [dot(part, source, 1, 0).astype(BF16) for part in parts]

    def dispatch(parts):
        got = [flip(part, SPLIT * k) for k, part in enumerate(parts, 1)]
        return got[0] if experts == 2 else jnp.concatenate(got, axis=0)

    near_x, *far_x = pick(tokens)
    near_u, *far_u = pick(scaled)
    gate, up, down = w_gate[0], w_up[0], w_down[0]
    gate_b, up_b = flip(gate, WEIGHT_BIT), flip(up, WEIGHT_BIT)

    far_x = dispatch(far_x)
    near_x2 = flip(near_x, ROW_BIT)
    far_x, near_x2, near_u, gate_b, *far_u = lax.optimization_barrier(
        (far_x, near_x2, near_u, gate_b, *far_u)
    )
    up_b, down_send = lax.optimization_barrier((up_b, down))
    far_u = dispatch(far_u)
    far_x2 = flip(far_x, ROW_BIT)
    down_b = flip(down_send, WEIGHT_BIT)
    near_x = jnp.concatenate([near_x, near_x2], axis=0)
    far_x2, near_p = lax.optimization_barrier((far_x2, near_x[:, :shared]))
    near_p = flip(near_p, WEIGHT_BIT)
    far_u2 = flip(far_u, ROW_BIT)
    far_x = jnp.concatenate([far_x, far_x2], axis=0)
    near_u, down_b, far_u2, near_p, far_p = lax.optimization_barrier(
        (near_u, down_b, far_u2, near_p, far_x[:, :shared])
    )
    far_p = flip(far_p, WEIGHT_BIT)
    near_u2 = flip(near_u, ROW_BIT)

    far_x = share_core(far_x)
    far_u = share_core(jnp.concatenate([far_u, far_u2], axis=0))
    near_x = share_core(near_x)

    gate = jnp.concatenate([gate, gate_b], axis=1)
    up = jnp.concatenate([up, up_b], axis=1)
    down = jnp.concatenate([down, down_b], axis=0)

    def hidden_pass(x, u):
        gate_pre = dot(x, gate, 1, 0)
        up_pre = dot(x, up, 1, 0)
        grad_act = dot(u, down, 1, 1)
        sigma = jax.nn.sigmoid(gate_pre)
        act_silu = gate_pre * sigma
        hidden = act_silu * up_pre
        prob = jnp.sum(hidden * grad_act, axis=1, keepdims=True).astype(BF16)
        grad_gpre = (grad_act * up_pre * sigma * (1.0 + gate_pre * (1.0 - sigma))).astype(BF16)
        grad_upre = (grad_act * act_silu).astype(BF16)
        return hidden.astype(BF16), grad_gpre, grad_upre, prob

    def rows_pass(grad_gpre, grad_upre, prob):
        rows = (dot(grad_gpre, gate, 1, 1) + dot(grad_upre, up, 1, 1)).astype(BF16)
        return jnp.concatenate([rows, jnp.broadcast_to(prob, (rows.shape[0], 128))], axis=1)

    far = hidden_pass(far_x, far_u)
    far_rows, near_u2, far_p = lax.optimization_barrier((rows_pass(*far[1:]), near_u2, far_p))
    near_u = share_core(jnp.concatenate([near_u, near_u2], axis=0))
    far_rows = sum_rows(far_rows)
    back = [
        flip(far_rows[(k - 1) * capacity : k * capacity], SPLIT * k) for k in range(1, experts)
    ]
    near = hidden_pass(near_x, near_u)
    near_rows = sum_rows(rows_pass(*near[1:]))

    x = jnp.concatenate([near_x, far_x], axis=0)
    u = jnp.concatenate([near_u, far_u], axis=0)
    hidden, grad_gpre, grad_upre = (
        jnp.concatenate([a, b], axis=0) for a, b in zip(near[:3], far[:3])
    )
    both = jnp.concatenate([grad_gpre[:, :hid], grad_upre[:, :hid]], axis=1)
    both_p = jnp.concatenate([grad_gpre[:, hid:], grad_upre[:, hid:]], axis=1)
    got_both = flip(both_p, WEIGHT_BIT)
    rest_p = dot(x[:, shared:], both_p, 0, 0).astype(BF16)
    down_p = dot(hidden[:, hid:], u, 0, 0).astype(BF16)
    x_p = jnp.concatenate([near_p, far_p], axis=0)
    rest_p, down_p, x_p = lax.optimization_barrier((rest_p, down_p, x_p))
    x_p_core = flip(x_p, CORE)
    at = x_p.shape[0] // 2
    x_p = jnp.concatenate([x_p[:at], x_p_core[:at], x_p[at:], x_p_core[at:]], axis=0)
    got_rest = flip(rest_p, WEIGHT_BIT)
    got_down = flip(down_p, WEIGHT_BIT)

    slot_rows = jnp.concatenate([near_rows] + back, axis=0)
    out = dot(select, slot_rows, 0, 0)
    grad_tokens = out[:, :features].astype(BF16)
    grad_combine = out[:, features : features + 1] / weight

    first = (dot(x[:, :shared], both, 0, 0) + dot(x_p, got_both, 0, 0)).astype(BF16)
    got_down, first = lax.optimization_barrier((got_down, first))
    grad_down = (dot(hidden[:, :hid], u, 0, 0) + got_down.astype(F32)).astype(BF16)[None]
    got_rest, first, grad_tokens, grad_combine, grad_down = lax.optimization_barrier(
        (got_rest, first, grad_tokens, grad_combine, grad_down)
    )
    rest = (dot(x[:, shared:], both, 0, 0) + got_rest.astype(F32)).astype(BF16)
    grad_gate, grad_up = (
        jnp.concatenate([first[:, at], rest[:, at]], axis=0)[None]
        for at in (slice(0, hid), slice(hid, None))
    )
    return (grad_tokens, grad_combine, grad_gate, grad_up, grad_down)


def solution(mesh):
    rows = P(("groups", "expert"), None)
    blocks = P(("groups", "expert"), None, None)
    weights = P("expert", None, None)
    return jax.shard_map(
        on_device,
        mesh=mesh,
        in_specs=(rows, rows, rows, rows, weights, weights, weights),
        out_specs=(rows, rows, blocks, blocks, blocks),
        check_vma=False,
    )
```

```python
import jax
import jax.numpy as jnp
from jax import lax
from jax.sharding import PartitionSpec as P

SPLIT = 8
CORE = 1
WEIGHT_BIT = 2
ROW_BIT = 4
SHARED_PART = 3

F32 = jnp.float32
BF16 = jnp.bfloat16


def dot(a, b, ca, cb):
    return lax.dot_general(a, b, (((ca,), (cb,)), ((), ())), preferred_element_type=F32)


def flip(x, mask):
    n = lax.axis_size("expert")
    return lax.ppermute(x, "expert", [(i, i ^ mask) for i in range(n)])


def add(a, b):
    return (a.astype(F32) + b.astype(F32)).astype(BF16)


def after(x, *others):
    return lax.optimization_barrier((x,) + others)[0]


def share_core(pair):
    return jnp.concatenate([pair, flip(pair, CORE)], axis=0)


def sum_rows(p):
    half = p.shape[0] // 2
    p = add(p[:half], flip(p[half:], CORE))
    half = half // 2
    return add(p[:half], flip(p[half:], ROW_BIT))


def on_device(tokens, grad_out, route_weight, expert_ids, w_gate, w_up, w_down):
    axis_count = lax.axis_size("expert")
    experts = axis_count // SPLIT
    tok_rows, features = tokens.shape
    hid = w_gate.shape[2]
    shared = features * SHARED_PART // 7 // 128 * 128
    capacity = min(tok_rows, 5 * tok_rows // (4 * experts))
    capacity = -(-capacity // 16) * 16
    mine = lax.axis_index("expert") // SPLIT

    relative = expert_ids[:, 0] ^ mine
    onehot = (relative[:, None] == jnp.arange(experts, dtype=jnp.int32)[None, :]).astype(BF16)
    earlier = (jnp.arange(tok_rows)[:, None] > jnp.arange(tok_rows)[None, :]).astype(BF16)
    before = dot(earlier, onehot, 1, 0)
    position = jnp.sum(before * onehot.astype(F32), axis=1).astype(jnp.int32)
    slot = relative * capacity + position
    select = (jnp.arange(experts * capacity, dtype=jnp.int32)[:, None] == slot[None, :]).astype(BF16)

    weight = route_weight.astype(F32)
    scaled = (weight * grad_out.astype(F32)).astype(BF16)

    def pick(source):
        parts = [select[k * capacity : (k + 1) * capacity] for k in range(experts)]
        return [dot(part, source, 1, 0).astype(BF16) for part in parts]

    def dispatch(parts):
        got = [flip(part, SPLIT * k) for k, part in enumerate(parts, 1)]
        return got[0] if experts == 2 else jnp.concatenate(got, axis=0)

    near_x, *far_x = pick(tokens)
    near_u, *far_u = pick(scaled)
    gate, up, down = w_gate[0], w_up[0], w_down[0]
    gate_b, up_b = flip(gate, WEIGHT_BIT), flip(up, WEIGHT_BIT)

    far_x = dispatch(far_x)
    near_x2 = flip(near_x, ROW_BIT)
    far_x, near_x2, near_u, gate_b, *far_u = lax.optimization_barrier(
        (far_x, near_x2, near_u, gate_b, *far_u)
    )
    up_b, down_send = lax.optimization_barrier((up_b, down))
    far_u = dispatch(far_u)
    far_x2 = flip(far_x, ROW_BIT)
    down_b = flip(down_send, WEIGHT_BIT)
    near_x = jnp.concatenate([near_x, near_x2], axis=0)
    far_x2, near_p = lax.optimization_barrier((far_x2, near_x[:, :shared]))
    near_p = flip(near_p, WEIGHT_BIT)
    far_u2 = flip(far_u, ROW_BIT)
    far_x = jnp.concatenate([far_x, far_x2], axis=0)
    near_u, down_b, far_u2, near_p, far_p = lax.optimization_barrier(
        (near_u, down_b, far_u2, near_p, far_x[:, :shared])
    )
    far_p = flip(far_p, WEIGHT_BIT)
    near_u2 = flip(near_u, ROW_BIT)

    far_x = share_core(far_x)
    far_u = share_core(jnp.concatenate([far_u, far_u2], axis=0))
    near_x = share_core(near_x)

    gate = jnp.concatenate([gate, gate_b], axis=1)
    up = jnp.concatenate([up, up_b], axis=1)
    down = jnp.concatenate([down, down_b], axis=0)

    def hidden_pass(x, u):
        gate_pre = dot(x, gate, 1, 0)
        up_pre = dot(x, up, 1, 0)
        grad_act = dot(u, down, 1, 1)
        sigma = jax.nn.sigmoid(gate_pre)
        act_silu = gate_pre * sigma
        hidden = act_silu * up_pre
        prob = jnp.sum(hidden * grad_act, axis=1, keepdims=True).astype(BF16)
        grad_gpre = (grad_act * up_pre * sigma * (1.0 + gate_pre * (1.0 - sigma))).astype(BF16)
        grad_upre = (grad_act * act_silu).astype(BF16)
        return hidden.astype(BF16), grad_gpre, grad_upre, prob

    def rows_pass(grad_gpre, grad_upre, prob):
        rows = (dot(grad_gpre, gate, 1, 1) + dot(grad_upre, up, 1, 1)).astype(BF16)
        return jnp.concatenate([rows, jnp.broadcast_to(prob, (rows.shape[0], 128))], axis=1)

    far = hidden_pass(far_x, far_u)
    far_rows, near_u2, far_p = lax.optimization_barrier((rows_pass(*far[1:]), near_u2, far_p))
    near_u = share_core(jnp.concatenate([near_u, near_u2], axis=0))
    far_rows = sum_rows(far_rows)
    back = [
        flip(far_rows[(k - 1) * capacity : k * capacity], SPLIT * k) for k in range(1, experts)
    ]
    near = hidden_pass(near_x, near_u)
    near_rows = sum_rows(rows_pass(*near[1:]))

    x = jnp.concatenate([near_x, far_x], axis=0)
    u = jnp.concatenate([near_u, far_u], axis=0)
    hidden, grad_gpre, grad_upre = (
        jnp.concatenate([a, b], axis=0) for a, b in zip(near[:3], far[:3])
    )
    both = jnp.concatenate([grad_gpre[:, :hid], grad_upre[:, :hid]], axis=1)
    both_p = jnp.concatenate([grad_gpre[:, hid:], grad_upre[:, hid:]], axis=1)
    got_both = flip(both_p, WEIGHT_BIT)
    rest_p = dot(x[:, shared:], both_p, 0, 0).astype(BF16)
    down_p = dot(hidden[:, hid:], u, 0, 0).astype(BF16)
    x_p = jnp.concatenate([near_p, far_p], axis=0)
    rest_p, down_p, x_p = lax.optimization_barrier((rest_p, down_p, x_p))
    x_p_core = flip(x_p, CORE)
    at = x_p.shape[0] // 2
    x_p = jnp.concatenate([x_p[:at], x_p_core[:at], x_p[at:], x_p_core[at:]], axis=0)
    got_rest = flip(rest_p, WEIGHT_BIT)
    got_down = flip(down_p, WEIGHT_BIT)

    slot_rows = jnp.concatenate([near_rows] + back, axis=0)
    grad_tokens = dot(select, slot_rows[:, :features], 0, 0).astype(BF16)
    prob = dot(slot_rows[:, features:], select, 0, 0)[:1]
    grad_combine = (prob / weight.reshape(1, tok_rows)).reshape(tok_rows, 1)

    first = (dot(x[:, :shared], both, 0, 0) + dot(x_p, got_both, 0, 0)).astype(BF16)
    got_down, first = lax.optimization_barrier((got_down, first))
    grad_down = (dot(hidden[:, :hid], u, 0, 0) + got_down.astype(F32)).astype(BF16)[None]
    got_rest, first, grad_tokens, grad_combine, grad_down = lax.optimization_barrier(
        (got_rest, first, grad_tokens, grad_combine, grad_down)
    )
    rest = (dot(x[:, shared:], both, 0, 0) + got_rest.astype(F32)).astype(BF16)
    grad_gate, grad_up = (
        jnp.concatenate([first[:, at], rest[:, at]], axis=0)[None]
        for at in (slice(0, hid), slice(hid, None))
    )
    return (grad_tokens, grad_combine, grad_gate, grad_up, grad_down)


def solution(mesh):
    rows = P(("groups", "expert"), None)
    blocks = P(("groups", "expert"), None, None)
    weights = P("expert", None, None)
    return jax.shard_map(
        on_device,
        mesh=mesh,
        in_specs=(rows, rows, rows, rows, weights, weights, weights),
        out_specs=(rows, rows, blocks, blocks, blocks),
        check_vma=False,
    )
```
